32 devices in a mesh: dp: 8 (over y, x, core), expert: 4 (over z).
Axes of the slice: x: 2, y: 2, z: 4, core: 2. Of those that a mesh axis runs over, the one named last changes fastest.
Arguments:
- tokens: bfloat16 [1024, 6144], P('dp'), may hold values from -6 to 6
- routes: int32 [1024, 2], P('dp'), may hold values from 0 to 3, all different within a row; in each aligned block of 128 rows (0 to 127, 128 to 255, ...) at most 128 rows name the same one
- gates: float32 [1024, 2], P('dp'), may hold values from 0.1 to 1
- capacity: int32 [4], replicated, may hold values from 64 to 128, as said below
- w_gate: bfloat16 [4, 6144, 8192], P('expert', None, 'dp'), may hold values from -0.078125 to 0.078125
- w_up: bfloat16 [4, 6144, 8192], P('expert', None, 'dp'), may hold values from -0.078125 to 0.078125
- w_down: bfloat16 [4, 8192, 6144], P('expert', 'dp'), may hold values from -0.0625 to 0.0625
Outputs:
- mixed: bfloat16 [1024, 6144], P('dp', 'expert')
The draws below stay inside these ranges and needn't reach their ends.
Inputs may be any that keep to these rules, and one draw needn't show every extreme that they name: `routes`: each token names two different experts. Within the 128 tokens of one index of dp no expert is named by more than 128 tokens, and in some shards one expert is named by exactly 128. Some expert's capacity is exactly 128.
All inputs are finite; a program needn't handle non-finite values.
Results may differ from the reference program's by a relative error of at most 0.015.
Values may be sent and summed in bfloat16 or wider, within the bound.
A program may use at most 128 MiB of HBM per device.

```python
import math
import jax
import jax.numpy as jnp
import numpy as np
from jax import lax

D = 6144
FF = 8192
TOK_DP = 128
EXPERTS = 4
CAP = 128
TOKENS = 1024
N_DP = 8


def draw_capacity(key, part):
    values = jax.random.randint(key, (EXPERTS,), CAP // 2, CAP + 1)
    picked = jax.random.randint(jax.random.fold_in(key, 7), (), 0, EXPERTS)
    return jnp.where(jnp.arange(EXPERTS) == picked, CAP, values).astype(jnp.int32)


def shard_levels(rng, extent, cuts, least, high):
    loudness = 1.0
    for dim, parts in cuts:
        draws = jax.random.uniform(jax.random.fold_in(jax.random.fold_in(rng, 6), dim), (parts,), jnp.float32, least / len(cuts), high / len(cuts))
        loudness = loudness * jnp.repeat(jnp.exp(draws), extent[dim] // parts).reshape((-1,) + (1,) * (len(extent) - 1 - dim))
    return loudness


def routed_block(own_key, own, number, rows, number_of, top, limit, lean):
    order = jax.random.permutation(own_key, number_of)
    packed, ordinary = load_shares(number_of, rows * top, limit, lean, True), load_shares(number_of, rows * top, limit, lean, False)
    places = jnp.arange(number_of)

    def named(sizes, turn):
        used = int((sizes > 0).sum())
        fixed = max(1, used // 4)
        shifted = fixed + (places - fixed + turn * (used - fixed)) % max(1, number_of - fixed)
        return jnp.zeros((number_of,), jnp.int32).at[order[jnp.where(places < fixed, places, shifted)]].set(jnp.asarray(sizes, jnp.int32))

    sizes = jnp.where(number % 4 == 0, named(packed, number // 4), named(ordinary, number - number // 4 - 1))
    mixed = jax.random.permutation(jax.random.fold_in(own, 3), number_of)
    source_of, taker = mixed[0:number_of // 2 * 2:2], mixed[1:number_of // 2 * 2:2]
    slack = jnp.minimum(sizes[source_of] - 1, limit - sizes[taker]) // 2
    slack = jnp.where((source_of == order[0]) | (taker == order[0]) | (sizes[taker] == 0), 0, jnp.maximum(slack, 0))
    shifted = jax.random.randint(jax.random.fold_in(own, 4), (number_of // 2,), 0, 1 << 20) % (slack + 1)
    sizes = sizes.at[source_of].add(-shifted).at[taker].add(shifted)
    items = jnp.searchsorted(jnp.cumsum(sizes), jnp.arange(rows * top), side="right").astype(jnp.int32)
    table = items.reshape(top, rows).T
    table = table[jax.random.permutation(jax.random.fold_in(own, 1), rows)]
    turn = jax.random.randint(jax.random.fold_in(own, 2), (rows, 1), 0, top)
    return jnp.take_along_axis(table, (jnp.arange(top)[None, :] + turn) % top, axis=1)


def load_shares(amount, total, reach, slope, full):
    portions = [(1 << 20) // math.isqrt(rank ** slope) + 1 for rank in range(1, amount + 1)]
    largest = reach if full else min(reach, max(-(-total // amount), total * portions[0] // sum(portions)))
    least = 1 if total - largest >= amount - 1 else 0
    given, rest = [largest] + [least] * (amount - 1), total - largest - least * (amount - 1)
    while rest > 0:
        candidates = [i for i in range(1, amount) if given[i] < largest] or [i for i in range(1, amount) if given[i] < reach]
        mass, remaining = sum([portions[i] for i in candidates]), rest
        for i in candidates:
            extra = min(reach - given[i], max(1, remaining * portions[i] // mass), rest)
            given[i] = given[i] + extra
            rest = rest - extra
    return np.array(given)


def noise(rng, shape, deviation, bound, cuts=(), kind=jnp.bfloat16):
    gain = shard_levels(rng, shape, cuts, -0.22, 0.18) if cuts else 1.0
    array = jax.random.normal(rng, shape, jnp.float32) * deviation * gain
    return jnp.minimum(jnp.maximum(array, -bound), bound).astype(kind)


def setup_inputs(seed: int = 0) -> dict:
    key_list = jax.random.split(jax.random.key(seed), 8)
    tokens = noise(key_list[0], (TOKENS, D), 1.0, 6.0, ((0, 8),))
    routes_keys = jax.random.split(jax.random.fold_in(key_list[1], 1), TOKENS // TOK_DP)
    routes_turns = jax.random.permutation(jax.random.fold_in(key_list[1], 3), TOKENS // TOK_DP)
    routes = jax.vmap(lambda own, number: routed_block(jax.random.fold_in(key_list[1], 2), own, number, TOK_DP, EXPERTS, 2, CAP, 2))(routes_keys, routes_turns).reshape((TOKENS, 2))
    gates = jnp.clip(0.1 + 0.9 * jax.random.uniform(key_list[2], (TOKENS, 2), jnp.float32) ** shard_levels(key_list[2], (TOKENS, 2), ((0, 8),), -0.2, 0.2), 0.1, 1.0)
    capacity = draw_capacity(jax.random.fold_in(key_list[7], 71), 0)
    w_gate = noise(key_list[4], (EXPERTS, D, FF), D ** -0.5, 0.078125, ((0, 4), (2, 8)))
    w_up = noise(key_list[5], (EXPERTS, D, FF), D ** -0.5, 0.078125, ((0, 4), (2, 8)))
    w_down = noise(key_list[6], (EXPERTS, FF, D), FF ** -0.5, 0.0625, ((0, 4), (1, 8)))
    return dict(tokens=tokens, routes=routes, gates=gates, capacity=capacity, w_gate=w_gate, w_up=w_up, w_down=w_down)


def reference(tokens, routes, gates, capacity, w_gate, w_up, w_down):
    shards = tokens.reshape(N_DP, TOK_DP, D)
    chosen = routes.reshape(N_DP, TOK_DP, 2)
    weights_all = gates.reshape(N_DP, TOK_DP, 2)
    slot_ids = jnp.arange(CAP, dtype=jnp.int32)
    panel_width = FF // N_DP
    accumulated = jnp.zeros((N_DP, TOK_DP, D), jnp.float32)
    for expert_id in range(EXPERTS):
        matched = chosen == expert_id
        member = jnp.any(matched, axis=-1).astype(jnp.int32)
        weight = jnp.sum(jnp.where(matched, weights_all, 0.0), axis=-1).astype(jnp.float32)
        position = jnp.cumsum(member, axis=1).astype(jnp.int32) - member
        retained = (member == 1) & (position < capacity[expert_id])
        selector = (retained[:, None, :] & (position[:, None, :] == slot_ids[None, :, None])).astype(jnp.float32)
        slot_rows = jnp.einsum("nct,ntd->ncd", selector, shards.astype(jnp.float32),
                               precision=lax.Precision.HIGHEST).astype(jnp.bfloat16)
        flat_rows = slot_rows.reshape(N_DP * CAP, D)
        gate_act = jnp.dot(flat_rows, w_gate[expert_id], preferred_element_type=jnp.float32)
        up_act = jnp.dot(flat_rows, w_up[expert_id], preferred_element_type=jnp.float32)
        hidden = (jax.nn.silu(gate_act) * up_act).astype(jnp.bfloat16)
        expert_out = jnp.zeros((N_DP * CAP, D), jnp.float32)
        for panel in range(N_DP):
            partial_value = jnp.dot(hidden[:, panel * panel_width:(panel + 1) * panel_width],
                              w_down[expert_id, panel * panel_width:(panel + 1) * panel_width, :],
                              preferred_element_type=jnp.float32).astype(jnp.bfloat16)
            partial_value = lax.optimization_barrier(partial_value)
            expert_out = expert_out + partial_value.astype(jnp.float32)
        placed = jnp.einsum("nct,ncd->ntd", selector, expert_out.reshape(N_DP, CAP, D),
                            precision=lax.Precision.HIGHEST)
        accumulated = accumulated + weight[:, :, None] * placed
    return accumulated.reshape(TOKENS, D).astype(jnp.bfloat16)
```

```python
import jax
import jax.numpy as jnp
from jax import lax
from jax.experimental import pallas as pl
from jax.experimental.pallas import tpu as pltpu
from jax.sharding import PartitionSpec as P

MESH = pl.DeviceIdType.MESH
CHIPS = 4
STEPS = 4


def keep_weight(routes, gates, capacity, owner, num_experts):
    matched = routes == owner
    member = jnp.any(matched, axis=-1).astype(jnp.int32)
    weight = jnp.sum(jnp.where(matched, gates, 0.0), axis=-1)
    rows = routes.shape[0]
    order = jnp.arange(rows, dtype=jnp.int32)
    before = order[None, :] < order[:, None]
    position = jnp.sum(jnp.where(before, member[None, :], 0), axis=-1)
    limit_value = jnp.sum(
        jnp.where(jnp.arange(num_experts, dtype=jnp.int32) == owner, capacity, 0)
    )
    retained = (member == 1) & (position < limit_value)
    return retained, position, weight


def fused(tok, wt, wg_hbm, wu_hbm, wd_hbm, out, x, wg, wu, wd, h, c, r, zr,
          load_sem, wd_sem, ag_send, ag_recv, fw_send, fw_recv, sib_send, sib_recv,
          rs_send, rs_recv, z_send, z_recv):
    rows, width = tok.shape
    quarter = width // STEPS
    hidden = wg.shape[1]
    half = rows // 2
    me = lax.axis_index("dp")
    z = lax.axis_index("expert")
    core = lax.rem(me, 2)
    cx = lax.rem(me // 2, 2)
    cy = me // 4
    sibling = (me - core + (1 - core), z)

    def chip(g):
        return ((lax.rem(cy + g // 2, 2) * 2 + lax.rem(cx + g % 2, 2)) * 2 + core, z)

    def peer(s):
        return (me, lax.rem(z + s + 1, STEPS))

    def cols(s):
        return pl.ds(pl.multiple_of(lax.rem(z + s + 1, STEPS) * quarter, quarter), quarter)

    def remote(src, dst, ssem, rsem, device):
        return pltpu.make_async_remote_copy(
            src_ref=src, dst_ref=dst, send_sem=ssem, recv_sem=rsem,
            device_id=device, device_id_type=MESH)

    mine, other = pl.ds(0, rows), pl.ds(rows, rows)

    own = pltpu.make_async_copy(tok, x.at[0, mine], load_sem.at[0])
    own.start()
    load_g = pltpu.make_async_copy(wg_hbm, wg, load_sem.at[1])
    load_u = pltpu.make_async_copy(wu_hbm, wu, load_sem.at[2])
    load_g.start()
    load_u.start()

    def wd_copy(s, slot):
        return pltpu.make_async_copy(wd_hbm.at[:, cols(s)], wd.at[slot], wd_sem.at[slot])

    barrier = pltpu.get_barrier_semaphore()
    partners = [sibling, chip(1), chip(2), chip(3), peer(0), peer(1), peer(2)]
    for p in partners:
        pl.semaphore_signal(barrier, inc=1, device_id=p, device_id_type=MESH)
    pl.semaphore_wait(barrier, len(partners))

    gather = [
        remote(tok, x.at[1, mine], ag_send.at[1], ag_recv.at[1], chip(1)),
        remote(tok, x.at[2, mine], ag_send.at[2], ag_recv.at[2], chip(2)),
        remote(tok, x.at[0, other], fw_send.at[0], fw_recv.at[0], sibling),
    ]
    for copy in gather:
        copy.start()
    wd_copy(0, 0).start()
    wd_copy(1, 1).start()

    def forward(g):
        return remote(x.at[g, mine], x.at[g, other], fw_send.at[g], fw_recv.at[g], sibling)

    def sib_copy(g, s):
        return remote(x.at[g, other, cols(s)], c.at[g, :, cols(s)],
                      sib_send.at[g, s], sib_recv.at[g, s], sibling)

    def rs_copy(g, s):
        return remote(x.at[g, mine, cols(s)], r.at[g - 1, :, cols(s)],
                      rs_send.at[g - 1, s], rs_recv.at[g - 1, s], chip(g))

    def gate_up(g):
        tile = 256

        def body(n, carry):
            where = pl.ds(pl.multiple_of(n * tile, tile), tile)
            a = jnp.dot(x[g], wg[:, where], preferred_element_type=jnp.float32)
            b = jnp.dot(x[g], wu[:, where], preferred_element_type=jnp.float32)
            h[:, where] = (a / (1.0 + jnp.exp(-a)) * b).astype(jnp.bfloat16)
            return carry

        lax.fori_loop(0, hidden // tile, body, 0)

    def chip_sum(g, s):
        sib_copy(g, s).wait_recv()
        if g > 0:
            tile = 16

            def body(i, carry):
                at = pl.ds(pl.multiple_of(i * tile, tile), tile)
                x[g, at, cols(s)] = (
                    x[g, at, cols(s)].astype(jnp.float32)
                    + c[g, at, cols(s)].astype(jnp.float32)).astype(jnp.bfloat16)
                return carry

            lax.fori_loop(0, rows // tile, body, 0)
            rs_copy(g, s).start()

    def down(g):
        tile = 256

        def step(s, carry):
            slot = lax.rem(s, 2)
            wd_copy(s, slot).wait()
            base = lax.rem(z + s + 1, STEPS) * quarter

            def body(n, inner):
                where = pl.ds(pl.multiple_of(n * tile, tile), tile)
                to = pl.ds(pl.multiple_of(base + n * tile, tile), tile)
                x[g, :, to] = jnp.dot(
                    h[...], wd[slot, :, where], preferred_element_type=jnp.float32
                ).astype(jnp.bfloat16)
                return inner

            lax.fori_loop(0, quarter // tile, body, 0)
            sib_copy(g, s).start()
            if g < CHIPS - 1:
                wd_copy(lax.rem(s + 2, STEPS), slot).start()
            else:
                @pl.when(s + 2 < STEPS)
                def _():
                    wd_copy(s + 2, slot).start()

            @pl.when(s > 0)
            def _():
                chip_sum(g, s - 1)

            return carry

        lax.fori_loop(0, STEPS, step, 0)
        chip_sum(g, STEPS - 1)

    own.wait()
    load_g.wait()
    load_u.wait()
    gather[2].wait()
    gate_up(0)
    down(0)

    gather[0].wait_recv()
    via_y = remote(x.at[1, pl.ds(0, half)], x.at[3, pl.ds(0, half)],
                   ag_send.at[3], ag_recv.at[3], chip(2))
    via_y.start()
    forward(1).start()
    gather[1].wait_recv()
    via_x = remote(x.at[2, pl.ds(half, half)], x.at[3, pl.ds(half, half)],
                   ag_send.at[0], ag_recv.at[0], chip(1))
    via_x.start()
    forward(2).start()
    forward(1).wait_recv()
    gate_up(1)
    via_y.wait_send()
    forward(1).wait_send()
    down(1)
    forward(2).wait_recv()
    gate_up(2)
    via_y.wait_recv()
    via_x.wait()
    forward(3).start()
    forward(2).wait_send()
    down(2)
    forward(3).wait()
    gate_up(3)
    down(3)

    def z_copy(s):
        return remote(x.at[0, mine, cols(s)], zr.at[s], z_send.at[s], z_recv.at[s], peer(s))

    tile = 16

    def total(s, at):
        value = x[0, at, cols(s)].astype(jnp.float32) + c[0, at, cols(s)].astype(jnp.float32)
        for g in range(1, CHIPS):
            value = value + r[g - 1, at, cols(s)].astype(jnp.float32)
        w = wt[at, 0:1]
        return jnp.where(w != 0.0, value * w, 0.0)

    def finish(s, carry):
        for g in range(1, CHIPS):
            rs_copy(g, s).wait_recv()

        def body(i, inner):
            at = pl.ds(pl.multiple_of(i * tile, tile), tile)
            x[0, at, cols(s)] = total(s, at).astype(jnp.bfloat16)
            return inner

        lax.fori_loop(0, rows // tile, body, 0)
        z_copy(s).start()
        return carry

    lax.fori_loop(0, STEPS - 1, finish, 0)
    last = STEPS - 1
    for g in range(1, CHIPS):
        rs_copy(g, last).wait_recv()
    for s in range(STEPS - 1):
        z_copy(s).wait_recv()

    def body(i, inner):
        at = pl.ds(pl.multiple_of(i * tile, tile), tile)
        value = total(last, at)
        for s in range(STEPS - 1):
            value = value + zr[s, at].astype(jnp.float32)
        out[at] = value.astype(jnp.bfloat16)
        return inner

    lax.fori_loop(0, rows // tile, body, 0)

    gather[0].wait_send()
    gather[1].wait_send()
    for s in range(STEPS):
        for g in range(CHIPS):
            sib_copy(g, s).wait_send()
            if g > 0:
                rs_copy(g, s).wait_send()
        if s < STEPS - 1:
            z_copy(s).wait_send()


def kernel_device(tokens, routes, gates, capacity, w_gate, w_up, w_down):
    rows, width = tokens.shape
    hidden = w_gate.shape[2]
    quarter = width // STEPS
    owner = lax.axis_index("expert")
    retained, _, weight = keep_weight(routes, gates, capacity, owner, capacity.shape[0])
    wt = jnp.broadcast_to(jnp.where(retained, weight, 0.0)[:, None], (rows, 128))
    any_space = pl.BlockSpec(memory_space=pl.ANY)
    vmem = pl.BlockSpec(memory_space=pltpu.VMEM)
    dma = pltpu.SemaphoreType.DMA
    return pl.pallas_call(
        fused,
        out_shape=jax.ShapeDtypeStruct((rows, quarter), jnp.bfloat16),
        in_specs=[any_space, vmem, any_space, any_space, any_space],
        out_specs=vmem,
        scratch_shapes=[
            pltpu.VMEM((CHIPS, 2 * rows, width), jnp.bfloat16),
            pltpu.VMEM((width, hidden), jnp.bfloat16),
            pltpu.VMEM((width, hidden), jnp.bfloat16),
            pltpu.VMEM((2, hidden, quarter), jnp.bfloat16),
            pltpu.VMEM((2 * rows, hidden), jnp.bfloat16),
            pltpu.VMEM((CHIPS, rows, width), jnp.bfloat16),
            pltpu.VMEM((CHIPS - 1, rows, width), jnp.bfloat16),
            pltpu.VMEM((STEPS - 1, rows, quarter), jnp.bfloat16),
            dma((3,)), dma((2,)),
            dma((CHIPS,)), dma((CHIPS,)), dma((CHIPS,)), dma((CHIPS,)),
            dma((CHIPS, STEPS)), dma((CHIPS, STEPS)),
            dma((CHIPS - 1, STEPS)), dma((CHIPS - 1, STEPS)),
            dma((STEPS - 1,)), dma((STEPS - 1,)),
        ],
        cost_estimate=pl.CostEstimate(
            flops=2 * 3 * 2 * CHIPS * rows * width * hidden,
            bytes_accessed=2 * (6 * hidden * width),
            transcendentals=2 * CHIPS * rows * hidden),
        compiler_params=pltpu.CompilerParams(
            collective_id=0, has_side_effects=True, vmem_limit_bytes=60 * 2**20),
    )(tokens, wt, w_gate[0], w_up[0], w_down[0])


def plain_device(tokens, routes, gates, capacity, w_gate, w_up, w_down):
    owner_index = lax.axis_index("expert")
    group_size = lax.axis_size("expert")
    local_rows = tokens.shape[0]
    num_experts = group_size * w_gate.shape[0]
    slot_count = 4 * local_rows // num_experts
    retained, position, weight = keep_weight(routes, gates, capacity, owner_index, num_experts)
    slot_ids = jnp.arange(slot_count, dtype=jnp.int32)
    selector = (retained[None, :] & (position[None, :] == slot_ids[:, None])).astype(jnp.bfloat16)
    slot_rows = jnp.dot(selector, tokens, preferred_element_type=jnp.float32).astype(jnp.bfloat16)
    block_rows = lax.all_gather(slot_rows, "dp", axis=0, tiled=True)
    gate_value = jnp.dot(block_rows, w_gate[0], preferred_element_type=jnp.float32)
    up_value = jnp.dot(block_rows, w_up[0], preferred_element_type=jnp.float32)
    hidden = (jax.nn.silu(gate_value) * up_value).astype(jnp.bfloat16)
    partial_value = jnp.dot(hidden, w_down[0], preferred_element_type=jnp.float32)
    returned = lax.psum_scatter(
        partial_value.astype(jnp.bfloat16), "dp", scatter_dimension=0, tiled=True
    ).astype(jnp.float32)
    placed = jnp.einsum(
        "ct,cd->td", selector.astype(jnp.float32), returned, precision=lax.Precision.HIGHEST
    )
    weighted = weight[:, None] * placed
    return lax.psum_scatter(
        weighted.astype(jnp.bfloat16), "expert", scatter_dimension=1, tiled=True
    )


def solution(mesh):
    in_specs = (
        P("dp", None),
        P("dp", None),
        P("dp", None),
        P(),
        P("expert", None, "dp"),
        P("expert", None, "dp"),
        P("expert", "dp", None),
    )
    fits = mesh.shape["dp"] == 2 * CHIPS and mesh.shape["expert"] == STEPS
    on_device = kernel_device if fits else plain_device
    return jax.shard_map(
        on_device, mesh=mesh, in_specs=in_specs, out_specs=P("dp", "expert"), check_vma=False
    )
```
